32 devices in a mesh: seq: 8 (over y, x, core), tp: 4 (over z).
Axes of the slice: x: 2, y: 2, z: 4, core: 2. Of those that a mesh axis runs over, the one named last changes fastest.
Arguments:
- patches: bfloat16 [4096, 1280], P('seq'), may hold values from -6 to 6
- image_ids: int32 [1024], replicated, may hold values from 0 to 15, never falling along the last dimension, each value on 1 to 128 neighbouring positions
- vision_gain: float32 [1280], replicated, may hold values from 0.5 to 2
- v_query: bfloat16 [1280, 1280], P(None, 'tp'), may hold values from -0.15625 to 0.15625
- v_key: bfloat16 [1280, 1280], P(None, 'tp'), may hold values from -0.15625 to 0.15625
- v_value: bfloat16 [1280, 1280], P(None, 'tp'), may hold values from -0.15625 to 0.15625
- v_out: bfloat16 [1280, 1280], P('tp'), may hold values from -0.625 to 0.625
- merge_gain: float32 [1280], replicated, may hold values from 0.5 to 1.5
- merge_up: bfloat16 [5120, 5120], P('seq', 'tp'), may hold values from -0.078125 to 0.078125
- merge_down: bfloat16 [5120, 8192], P('tp', 'seq'), may hold values from -0.078125 to 0.078125
- owners: int32 [1024, 1], replicated, may hold values from 0 to 7; in each aligned block of 128 rows (0 to 127, 128 to 255, ...) at most 32 rows name the same one
- text_embed: bfloat16 [2048, 8192], P('seq', 'tp'), may hold values from -6 to 6
- segment_ids: int32 [2048], P('seq'), may hold values from 0 to 31, never falling along the last dimension, each value on 1 to 256 neighbouring positions
- lang_gain: float32 [8192], replicated, may hold values from 0.5 to 2
- l_query: bfloat16 [8192, 4096], P(None, 'tp'), may hold values from -0.0625 to 0.0625
- l_key: bfloat16 [8192, 1024], P(None, 'tp'), may hold values from -0.0625 to 0.0625
- l_value: bfloat16 [8192, 1024], P(None, 'tp'), may hold values from -0.0625 to 0.0625
- l_out: bfloat16 [4096, 8192], P('tp'), may hold values from -0.09375 to 0.09375
Outputs:
- layer_out: bfloat16 [2048, 8192], P('seq', 'tp')
The draws below stay inside these ranges and needn't reach their ends.
Inputs may be any that keep to these rules, and one draw needn't show every extreme that they name: `image_ids`: never falling; each image spans 1 to 128 merged tokens, one exactly 128. `owners`: among the rows of one device (aligned blocks of 128 rows) at most 32 name the same packed sequence. `segment_ids`: never falling; each document holds 1 to 256 slots, one exactly 256.
All inputs are finite; a program needn't handle non-finite values.
Results may differ from the reference program's by a relative error of at most 0.019.
Values may be sent and summed in bfloat16 or wider, within the bound.
A program may use at most 128 MiB of HBM per device.

```python
import math
import jax
import jax.numpy as jnp
import numpy as np
from jax import lax

DV = 1280
VHEADS = 16
MHID = 5120
D = 8192
LHEADS = 32
LKV = 8
LHD = 128
PAT_DEV = 512
MIN = 5120
QW = 4096
KW = 1024
MERGED_DEV = 128
CAP = 256
PAIR_CAP = 32
PATCHES = 4096
MERGED = 1024
SLOTS = 2048
IMAGES = 16
SEGS = 32
N_SEQ = 8
N_TP = 4


def gain_draw(key, width):
    return jax.random.uniform(key, (width,), jnp.float32, 0.6, 1.4)


def draw_vision_gain(key, part):
    return gain_draw(jax.random.fold_in(key, 11), DV)


def draw_lang_gain(key, part):
    return gain_draw(jax.random.fold_in(key, 23), D)


def steps_of(rng, dims, pieces, least, top_value):
    gain, own = 1.0, jax.random.fold_in(rng, 6)
    for axis_at, shards_of in pieces:
        steps = jnp.exp(jax.random.uniform(jax.random.fold_in(own, axis_at), (shards_of,), jnp.float32, least / len(pieces), top_value / len(pieces)))
        gain = gain * jnp.repeat(steps, dims[axis_at] // shards_of).reshape([-1 if axis == axis_at else 1 for axis in range(len(dims))])
    return gain


def split_up(amount, total, reach, slope):
    weights = [(1 << 20) // math.isqrt(rank ** slope) + 1 for rank in range(2, amount + 1)]
    rest, holding = total - reach - (amount - 1), [1] * (amount - 1)
    while rest > 0:
        movable = [i for i in range(amount - 1) if holding[i] < reach]
        pool, remaining = sum([weights[i] for i in movable]), rest
        for i in movable:
            addition = min(reach - holding[i], max(1, remaining * weights[i] // pool), rest)
            holding[i] = holding[i] + addition
            rest = rest - addition
    return np.array([reach] + holding)


def uneven(stream_key, number_of, total, bound, lean):
    if number_of == 2:
        one = jax.random.randint(stream_key, (), max(1, total - bound), min(bound, total - 1) + 1)
        return jnp.stack([one, total - one])
    tallies = jnp.asarray(split_up(number_of, total, bound, lean), jnp.int32)
    couples = (number_of - 1) // 2
    donor, sink = tallies[1:1 + 2 * couples:2], tallies[2:2 + 2 * couples:2]
    margin = jnp.minimum(donor - 1, bound - sink)
    shifted = jax.random.randint(jax.random.fold_in(stream_key, 1), (couples,), 0, 1 << 20) % (margin + 1)
    tallies = tallies.at[1:1 + 2 * couples:2].set(donor - shifted).at[2:2 + 2 * couples:2].set(sink + shifted)
    return tallies[jax.random.permutation(jax.random.fold_in(stream_key, 2), number_of)]


def routed_block(own_key, own, number, rows, number_of, top, reach, slope):
    ranking = jax.random.permutation(own_key, number_of)
    crowded, common = portions_of(number_of, rows * top, reach, slope, True), portions_of(number_of, rows * top, reach, slope, False)
    places = jnp.arange(number_of)

    def named(sizes, turn):
        used = int((sizes > 0).sum())
        fixed = max(1, used // 4)
        passed = fixed + (places - fixed + turn * (used - fixed)) % max(1, number_of - fixed)
        return jnp.zeros((number_of,), jnp.int32).at[ranking[jnp.where(places < fixed, places, passed)]].set(jnp.asarray(sizes, jnp.int32))

    sizes = jnp.where(number % 4 == 0, named(crowded, number // 4), named(common, number - number // 4 - 1))
    mixed = jax.random.permutation(jax.random.fold_in(own, 3), number_of)
    donor, sink = mixed[0:number_of // 2 * 2:2], mixed[1:number_of // 2 * 2:2]
    slack = jnp.minimum(sizes[donor] - 1, reach - sizes[sink]) // 2
    slack = jnp.where((donor == ranking[0]) | (sink == ranking[0]) | (sizes[sink] == 0), 0, jnp.maximum(slack, 0))
    passed = jax.random.randint(jax.random.fold_in(own, 4), (number_of // 2,), 0, 1 << 20) % (slack + 1)
    sizes = sizes.at[donor].add(-passed).at[sink].add(passed)
    labels = jnp.searchsorted(jnp.cumsum(sizes), jnp.arange(rows * top), side="right").astype(jnp.int32)
    grid = labels.reshape(top, rows).T
    grid = grid[jax.random.permutation(jax.random.fold_in(own, 1), rows)]
    turn = jax.random.randint(jax.random.fold_in(own, 2), (rows, 1), 0, top)
    return jnp.take_along_axis(grid, (jnp.arange(top)[None, :] + turn) % top, axis=1)


def portions_of(amount, total, limit, lean, full):
    portions = [(1 << 20) // math.isqrt(grade ** lean) + 1 for grade in range(1, amount + 1)]
    largest = limit if full else min(limit, max(-(-total // amount), total * portions[0] // sum(portions)))
    least = 1 if total - largest >= amount - 1 else 0
    given, surplus = [largest] + [least] * (amount - 1), total - largest - least * (amount - 1)
    while surplus > 0:
        movable = [i for i in range(1, amount) if given[i] < largest] or [i for i in range(1, amount) if given[i] < limit]
        pool, budget = sum([portions[i] for i in movable]), surplus
        for i in movable:
            extra = min(limit - given[i], max(1, budget * portions[i] // pool), surplus)
            given[i] = given[i] + extra
            surplus = surplus - extra
    return np.array(given)


def noise(key, dims, deviation, reach, pieces=(), kind=jnp.bfloat16):
    values = jax.random.normal(key, dims, jnp.float32) * deviation
    if len(pieces) > 0:
        values = steps_of(key, dims, pieces, -0.22, 0.18) * values
    return jnp.clip(values, min=-reach, max=reach).astype(kind)


def setup_inputs(seed: int = 0) -> dict:
    key_of = jax.random.split(jax.random.key(seed), 19)
    patches = noise(key_of[0], (PATCHES, DV), 1.0, 6.0, ((0, 8),))
    image_ids = jnp.searchsorted(jnp.cumsum(uneven(key_of[1], IMAGES, MERGED, MERGED_DEV, 2)), jnp.arange(MERGED), side="right").astype(jnp.int32)
    vision_gain = draw_vision_gain(jax.random.fold_in(key_of[18], 71), 0)
    v_query = noise(key_of[3], (DV, DV), DV ** -0.5, 0.15625, ((1, 4),))
    v_key = noise(key_of[4], (DV, DV), DV ** -0.5, 0.15625, ((1, 4),))
    v_value = noise(key_of[5], (DV, DV), DV ** -0.5, 0.15625, ((1, 4),))
    v_out = noise(key_of[6], (DV, DV), (DV // 16) ** -0.5, 0.625, ((0, 4),))
    merge_gain = jnp.clip(1.0 + 0.1 * jax.random.normal(key_of[7], (DV,), jnp.float32), 0.5, 1.5)
    merge_up = noise(key_of[8], (MIN, MHID), MIN ** -0.5, 0.078125, ((0, 8), (1, 4)))
    merge_down = noise(key_of[9], (MHID, D), MHID ** -0.5, 0.078125, ((0, 4), (1, 8)))
    owners_keys = jax.random.split(jax.random.fold_in(key_of[10], 1), MERGED // MERGED_DEV)
    owners_turns = jax.random.permutation(jax.random.fold_in(key_of[10], 3), MERGED // MERGED_DEV)
    owners = jax.vmap(lambda own, number: routed_block(jax.random.fold_in(key_of[10], 2), own, number, MERGED_DEV, N_SEQ, 1, PAIR_CAP, 2))(owners_keys, owners_turns).reshape((MERGED, 1))
    text_embed = noise(key_of[11], (SLOTS, D), 1.0, 6.0, ((0, 8), (1, 4)))
    segment_ids = jnp.searchsorted(jnp.cumsum(uneven(key_of[12], SEGS, SLOTS, CAP, 2)), jnp.arange(SLOTS), side="right").astype(jnp.int32)
    lang_gain = draw_lang_gain(jax.random.fold_in(key_of[18], 71), 0)
    l_query = noise(key_of[14], (D, QW), D ** -0.5, 0.0625, ((1, 4),))
    l_key = noise(key_of[15], (D, KW), D ** -0.5, 0.0625, ((1, 4),))
    l_value = noise(key_of[16], (D, KW), D ** -0.5, 0.0625, ((1, 4),))
    l_out = noise(key_of[17], (QW, D), QW ** -0.5, 0.09375, ((0, 4),))
    return {"patches": patches, "image_ids": image_ids, "vision_gain": vision_gain, "v_query": v_query, "v_key": v_key, "v_value": v_value, "v_out": v_out, "merge_gain": merge_gain, "merge_up": merge_up, "merge_down": merge_down, "owners": owners, "text_embed": text_embed, "segment_ids": segment_ids, "lang_gain": lang_gain, "l_query": l_query, "l_key": l_key, "l_value": l_value, "l_out": l_out}


EPSILON = 1e-06
NEG_FILL = -1e+30

def rms_scaled(values, norm_gain):
    mean_square = lax.optimization_barrier(jnp.mean(values * values, axis=-1, keepdims=True))
    return (values * lax.rsqrt(mean_square + EPSILON) * norm_gain).astype(jnp.bfloat16)

def narrowed(values):
    return lax.optimization_barrier(values.astype(jnp.bfloat16)).astype(jnp.float32)

def block_sum(left, right):
    width = left.shape[1] // N_TP
    totals = jnp.zeros((left.shape[0], right.shape[1]), jnp.float32)
    for block_index in range(N_TP):
        lower = block_index * width
        partial_value = jnp.dot(left[:, lower:lower + width], right[lower:lower + width], preferred_element_type=jnp.float32)
        totals = totals + narrowed(partial_value)
    return totals

def masked_mix(query_rows, key_rows, value_rows, allowed, score_scale):
    scores = jnp.einsum('qhd,nhd->hqn', query_rows, key_rows) * score_scale
    scores = jnp.where(allowed[None], scores, NEG_FILL)
    highest = lax.optimization_barrier(jnp.max(scores, axis=-1, keepdims=True))
    weights_raw = jnp.where(allowed[None], jnp.exp(scores - highest), 0.0)
    totals = lax.optimization_barrier(jnp.sum(weights_raw, axis=-1))
    mixed = jnp.einsum('hqn,nhd->qhd', narrowed(weights_raw), value_rows)
    return mixed / jnp.transpose(totals)[:, :, None]

def vision_attention(query_rows, key_rows, value_rows, patch_ids):
    head_size = DV // VHEADS
    score_scale = 1.0 / math.sqrt(head_size)
    padded_keys = jnp.pad(key_rows, ((PAT_DEV, PAT_DEV), (0, 0), (0, 0)))
    padded_values = jnp.pad(value_rows, ((PAT_DEV, PAT_DEV), (0, 0), (0, 0)))
    padded_ids = jnp.pad(patch_ids, (PAT_DEV, PAT_DEV), constant_values=-1)

    def one_block(block_index):
        first_row = (block_index * PAT_DEV).astype(jnp.int32)
        block_queries = lax.dynamic_slice_in_dim(query_rows, first_row, PAT_DEV, 0).astype(jnp.float32)
        block_keys = lax.dynamic_slice_in_dim(padded_keys, first_row, 3 * PAT_DEV, 0).astype(jnp.float32)
        block_values = lax.dynamic_slice_in_dim(padded_values, first_row, 3 * PAT_DEV, 0).astype(jnp.float32)
        query_ids = lax.dynamic_slice_in_dim(patch_ids, first_row, PAT_DEV, 0)
        key_ids = lax.dynamic_slice_in_dim(padded_ids, first_row, 3 * PAT_DEV, 0)
        allowed = query_ids[:, None] == key_ids[None, :]
        mixed = masked_mix(block_queries, block_keys, block_values, allowed, score_scale)
        return mixed.astype(jnp.bfloat16)
    blocks = lax.map(one_block, jnp.arange(N_SEQ, dtype=jnp.int32))
    return blocks.reshape(PATCHES, DV)

def language_attention(query_rows, key_rows, value_rows, segment_ids):
    group_size = LHEADS // LKV
    query_grid = query_rows.astype(jnp.float32).reshape(N_SEQ, CAP, LKV, group_size, LHD)
    key_grid = key_rows.astype(jnp.float32).reshape(N_SEQ, CAP, LKV, LHD)
    value_grid = value_rows.astype(jnp.float32).reshape(N_SEQ, CAP, LKV, LHD)
    segment_grid = segment_ids.reshape(N_SEQ, CAP)
    position = jnp.arange(CAP, dtype=jnp.int32)
    allowed = (segment_grid[:, :, None] == segment_grid[:, None, :]) & (position[None, None, :] <= position[None, :, None])
    scores = jnp.einsum('bqkgd,bnkd->bkgqn', query_grid, key_grid) / math.sqrt(LHD)
    scores = jnp.where(allowed[:, None, None], scores, NEG_FILL)
    highest = lax.optimization_barrier(jnp.max(scores, axis=-1, keepdims=True))
    weights_raw = jnp.where(allowed[:, None, None], jnp.exp(scores - highest), 0.0)
    totals = lax.optimization_barrier(jnp.sum(weights_raw, axis=-1))
    mixed = jnp.einsum('bkgqn,bnkd->bqkgd', narrowed(weights_raw), value_grid)
    mixed = mixed / jnp.transpose(totals, (0, 3, 1, 2))[..., None]
    return mixed.reshape(SLOTS, LHEADS * LHD).astype(jnp.bfloat16)

def reference(patches, image_ids, vision_gain, v_query, v_key, v_value, v_out, merge_gain, merge_up, merge_down, owners, text_embed, segment_ids, lang_gain, l_query, l_key, l_value, l_out):
    head_size = DV // VHEADS
    patch_ids = jnp.repeat(image_ids, 4)
    vision_state = patches.astype(jnp.float32)
    normed = rms_scaled(vision_state, vision_gain)
    query_rows = jnp.dot(normed, v_query, preferred_element_type=jnp.float32).astype(jnp.bfloat16).reshape(PATCHES, VHEADS, head_size)
    key_rows = jnp.dot(normed, v_key, preferred_element_type=jnp.float32).astype(jnp.bfloat16).reshape(PATCHES, VHEADS, head_size)
    value_rows = jnp.dot(normed, v_value, preferred_element_type=jnp.float32).astype(jnp.bfloat16).reshape(PATCHES, VHEADS, head_size)
    attended = vision_attention(query_rows, key_rows, value_rows, patch_ids)
    vision_state = vision_state + block_sum(attended, v_out)
    merge_input = rms_scaled(vision_state, merge_gain).reshape(MERGED, 4 * DV)
    hidden = jax.nn.gelu(jnp.dot(merge_input, merge_up, preferred_element_type=jnp.float32), approximate=False).astype(jnp.bfloat16)
    merged = block_sum(hidden, merge_down).astype(jnp.bfloat16)
    destination = owners[:, 0].astype(jnp.int32)
    one_hot = (destination[:, None] == jnp.arange(N_SEQ, dtype=jnp.int32)[None, :]).astype(jnp.int32)
    earlier = lax.optimization_barrier(jnp.sum((jnp.cumsum(one_hot, axis=0) - one_hot) * one_hot, axis=1))
    slot_index = (destination * CAP + earlier).astype(jnp.int32)
    filled = text_embed.at[slot_index].set(merged)
    lang_normed = rms_scaled(filled.astype(jnp.float32), lang_gain)
    lang_query = jnp.dot(lang_normed, l_query, preferred_element_type=jnp.float32).astype(jnp.bfloat16)
    lang_key = jnp.dot(lang_normed, l_key, preferred_element_type=jnp.float32).astype(jnp.bfloat16)
    lang_value = jnp.dot(lang_normed, l_value, preferred_element_type=jnp.float32).astype(jnp.bfloat16)
    lang_attended = language_attention(lang_query, lang_key, lang_value, segment_ids)
    return (filled.astype(jnp.float32) + block_sum(lang_attended, l_out)).astype(jnp.bfloat16)
```

```python
import math

import jax
import jax.numpy as jnp
from jax import lax
from jax.sharding import PartitionSpec as P

DV = 1280
VHEADS = 16
LHD = 128


EPSILON = 1e-06
NEG_FILL = -1e30


def extended(cells, sides, width):
    for axis, dim in sides:
        count = lax.axis_size(axis)
        ends = count - 1
        head = lax.slice_in_dim(cells, 0, width, axis=dim)
        tail = lax.slice_in_dim(cells, cells.shape[dim] - width, cells.shape[dim], axis=dim)
        cells = jnp.concatenate(
            [
                lax.ppermute(tail, axis, [(i, (i + 1) % count) for i in range(ends)]),
                cells,
                lax.ppermute(head, axis, [((i + 1) % count, i) for i in range(ends)]),
            ],
            axis=dim,
        )
    return cells


def rms_scaled(values, norm_gain):
    mean_square = jnp.mean(values * values, axis=-1, keepdims=True)
    return (values * lax.rsqrt(mean_square + EPSILON) * norm_gain).astype(jnp.bfloat16)


def masked_attend(query_rows, key_rows, value_rows, allowed, score_scale):
    scores = (
        jnp.einsum("qhd,nhd->hqn", query_rows, key_rows, preferred_element_type=jnp.float32)
        * score_scale
    )
    scores = jnp.where(allowed[None], scores, NEG_FILL)
    highest = jnp.max(scores, axis=-1, keepdims=True)
    weights_raw = jnp.where(allowed[None], jnp.exp(scores - highest), 0.0)
    totals = jnp.sum(weights_raw, axis=-1)
    mixed = jnp.einsum(
        "hqn,nhd->qhd",
        weights_raw.astype(jnp.bfloat16),
        value_rows,
        preferred_element_type=jnp.float32,
    )
    mixed = mixed / jnp.transpose(totals)[:, :, None]
    return mixed.reshape(mixed.shape[0], -1).astype(jnp.bfloat16)


def body(
    patches,
    image_ids,
    vision_gain,
    v_query,
    v_key,
    v_value,
    v_out,
    merge_gain,
    merge_up,
    merge_down,
    owners,
    text_embed,
    segment_ids,
    lang_gain,
    l_query,
    l_key,
    l_value,
    l_out,
):
    seq_count, tp_count = lax.axis_size("seq"), lax.axis_size("tp")
    seq_index, tp_index = lax.axis_index("seq"), lax.axis_index("tp")
    row_count = patches.shape[0]
    local_width = v_query.shape[1]
    head_size = DV // VHEADS
    head_count = local_width // head_size
    score_scale = 1.0 / math.sqrt(head_size)

    out_rows = v_out.shape[0] // seq_count
    v_out_whole = lax.all_gather(
        lax.dynamic_slice_in_dim(v_out, seq_index * out_rows, out_rows),
        ("tp", "seq"),
        axis=0,
        tiled=True,
    )
    text_rows = lax.all_gather(text_embed, "tp", axis=1, tiled=True)
    lang_rows = l_out.shape[0] // seq_count
    l_out_cut = lax.all_to_all(
        lax.dynamic_slice_in_dim(l_out, seq_index * lang_rows, lang_rows),
        "tp",
        split_axis=1,
        concat_axis=0,
        tiled=True,
    )
    l_out_columns = lax.all_gather(l_out_cut, "seq", axis=0, tiled=True)

    patch_ids = jnp.repeat(image_ids, 4)
    my_ids = lax.dynamic_slice_in_dim(patch_ids, seq_index * row_count, row_count)
    normed = rms_scaled(patches.astype(jnp.float32), vision_gain)
    query_rows = jnp.dot(normed, v_query, preferred_element_type=jnp.float32).astype(jnp.bfloat16)
    key_part = jnp.dot(normed, v_key, preferred_element_type=jnp.float32).astype(jnp.bfloat16)
    value_part = jnp.dot(normed, v_value, preferred_element_type=jnp.float32).astype(jnp.bfloat16)
    key_value = jnp.concatenate([key_part, value_part], axis=1)
    query_grid = query_rows.reshape(row_count, head_count, head_size)
    nearby = extended(key_value, (("seq", 0),), row_count)
    padded_ids = jnp.pad(patch_ids, (row_count, row_count), constant_values=-1)
    nearby_ids = lax.dynamic_slice_in_dim(padded_ids, seq_index * row_count, 3 * row_count)
    allowed = my_ids[:, None] == nearby_ids[None, :]
    nearby_keys = nearby[:, :local_width].reshape(3 * row_count, head_count, head_size)
    nearby_values = nearby[:, local_width:].reshape(3 * row_count, head_count, head_size)
    attended = masked_attend(query_grid, nearby_keys, nearby_values, allowed, score_scale)

    attended = lax.all_to_all(attended, "tp", split_axis=0, concat_axis=1, tiled=True)
    own_rows = row_count // tp_count
    own_patches = lax.dynamic_slice_in_dim(patches, tp_index * own_rows, own_rows)
    vision_state = own_patches.astype(jnp.float32) + jnp.dot(
        attended, v_out_whole, preferred_element_type=jnp.float32
    )
    merge_rows = rms_scaled(vision_state, merge_gain).reshape(own_rows // 4, 4 * DV)

    own_tokens = own_rows // 4
    spread = lax.all_to_all(merge_rows, "seq", split_axis=1, concat_axis=0, tiled=True)
    spread = lax.all_gather(spread, "tp", axis=0, tiled=True)
    spread = jnp.swapaxes(spread.reshape(tp_count, seq_count, own_tokens, -1), 0, 1)
    spread = spread.reshape(tp_count * seq_count * own_tokens, -1)
    up_terms = jnp.dot(spread, merge_up, preferred_element_type=jnp.float32)
    hidden_sum = lax.psum_scatter(
        up_terms.astype(jnp.bfloat16), "seq", scatter_dimension=0, tiled=True
    ).astype(jnp.float32)
    hidden = jax.nn.gelu(hidden_sum, approximate=False).astype(jnp.bfloat16)
    hidden = lax.all_gather(hidden, "seq", axis=0, tiled=True)
    down_terms = jnp.dot(hidden, merge_down, preferred_element_type=jnp.float32)
    merged = lax.psum_scatter(
        down_terms.astype(jnp.bfloat16), "tp", scatter_dimension=0, tiled=True
    )

    token_count = row_count // 4
    all_tokens = token_count * seq_count
    group = all_tokens // tp_count
    cap = (2 * token_count // seq_count) * (group // token_count)
    destination = owners[:, 0]
    one_hot = (
        destination[:, None] == jnp.arange(seq_count, dtype=jnp.int32)[None, :]
    ).astype(jnp.int32)
    grid_counts = one_hot.reshape(tp_count, group, seq_count)
    mine = lax.dynamic_slice_in_dim(grid_counts, tp_index, 1, 0)[0]
    rank = jnp.sum((jnp.cumsum(mine, axis=0) - mine) * mine, axis=1)
    send_index = lax.dynamic_slice_in_dim(destination, tp_index * group, group) * cap + rank
    send_place = jnp.arange(seq_count * cap, dtype=jnp.int32)[:, None] == send_index[None, :]
    outgoing = jnp.dot(
        send_place.astype(jnp.bfloat16), merged, preferred_element_type=jnp.float32
    ).astype(jnp.bfloat16)
    incoming = lax.all_to_all(
        outgoing.reshape(seq_count, cap, -1), "seq", split_axis=0, concat_axis=2, tiled=True
    )[0]
    arrived = lax.all_gather(incoming, "tp", axis=0, tiled=True)
    slot_count = text_embed.shape[0]
    group_counts = jnp.sum(grid_counts, axis=1)
    from_each = lax.dynamic_slice_in_dim(group_counts, seq_index, 1, 1)[:, 0]
    offsets = jnp.cumsum(from_each) - from_each
    cap_rank = jnp.arange(cap, dtype=jnp.int32)
    slot_of = jnp.where(
        cap_rank[None, :] < from_each[:, None], offsets[:, None] + cap_rank[None, :], slot_count
    ).reshape(-1)
    slots = jnp.arange(slot_count, dtype=jnp.int32)
    slot_place = slots[:, None] == slot_of[None, :]
    vision_slots = jnp.dot(
        slot_place.astype(jnp.bfloat16), arrived, preferred_element_type=jnp.float32
    ).astype(jnp.bfloat16)
    is_vision = slots < jnp.sum(from_each)
    full_rows = jnp.where(is_vision[:, None], vision_slots, text_rows)
    own_width = text_embed.shape[1]
    filled = lax.dynamic_slice_in_dim(full_rows, tp_index * own_width, own_width, axis=1)

    lang_normed = lax.optimization_barrier(
        rms_scaled(full_rows.astype(jnp.float32), lang_gain)
    )
    lang_query = jnp.dot(lang_normed, l_query, preferred_element_type=jnp.float32).astype(
        jnp.bfloat16
    )
    lang_key = jnp.dot(lang_normed, l_key, preferred_element_type=jnp.float32).astype(jnp.bfloat16)
    lang_value = jnp.dot(lang_normed, l_value, preferred_element_type=jnp.float32).astype(
        jnp.bfloat16
    )
    kv_heads = l_key.shape[1] // LHD
    group_size = l_query.shape[1] // LHD // kv_heads
    query_five = lang_query.reshape(slot_count, kv_heads, group_size, LHD)
    key_three = lang_key.reshape(slot_count, kv_heads, LHD)
    value_three = lang_value.reshape(slot_count, kv_heads, LHD)
    allowed_lang = (segment_ids[:, None] == segment_ids[None, :]) & (
        slots[None, :] <= slots[:, None]
    )
    scores = jnp.einsum(
        "qkgd,nkd->kgqn", query_five, key_three, preferred_element_type=jnp.float32
    ) / math.sqrt(LHD)
    scores = jnp.where(allowed_lang[None, None], scores, NEG_FILL)
    highest = jnp.max(scores, axis=-1, keepdims=True)
    weights_raw = jnp.where(allowed_lang[None, None], jnp.exp(scores - highest), 0.0)
    totals = jnp.sum(weights_raw, axis=-1)
    mixed = jnp.einsum(
        "kgqn,nkd->qkgd",
        weights_raw.astype(jnp.bfloat16),
        value_three,
        preferred_element_type=jnp.float32,
    )
    mixed = mixed / jnp.transpose(totals, (2, 0, 1))[..., None]
    lang_attended = mixed.reshape(slot_count, -1).astype(jnp.bfloat16)
    heads = lax.all_gather(lang_attended, "tp", axis=0)
    heads = heads.reshape(tp_count, slot_count, seq_count, lang_rows)
    heads = jnp.transpose(heads, (1, 2, 0, 3)).reshape(slot_count, -1)
    summed_out = jnp.dot(heads, l_out_columns, preferred_element_type=jnp.float32)
    return (filled.astype(jnp.float32) + summed_out).astype(jnp.bfloat16)


def solution(mesh):
    in_specs = (
        P("seq", None),
        P(),
        P(),
        P(None, "tp"),
        P(None, "tp"),
        P(None, "tp"),
        P("tp", None),
        P(),
        P("seq", "tp"),
        P("tp", "seq"),
        P(),
        P("seq", "tp"),
        P("seq"),
        P(),
        P(None, "tp"),
        P(None, "tp"),
        P(None, "tp"),
        P("tp", None),
    )
    out_specs = P("seq", "tp")
    return jax.shard_map(body, mesh=mesh, in_specs=in_specs, out_specs=out_specs, check_vma=False)
```

```python
import math

import jax
import jax.numpy as jnp
from jax import lax
from jax.experimental import pallas as pl
from jax.experimental.pallas import tpu as pltpu
from jax.sharding import PartitionSpec as P

DV = 1280
VHEADS = 16
LHD = 128


EPSILON = 1e-06
NEG_FILL = -1e30


def extended(cells, sides, width):
    for axis, dim in sides:
        count = lax.axis_size(axis)
        ends = count - 1
        head = lax.slice_in_dim(cells, 0, width, axis=dim)
        tail = lax.slice_in_dim(cells, cells.shape[dim] - width, cells.shape[dim], axis=dim)
        cells = jnp.concatenate(
            [
                lax.ppermute(tail, axis, [(i, (i + 1) % count) for i in range(ends)]),
                cells,
                lax.ppermute(head, axis, [((i + 1) % count, i) for i in range(ends)]),
            ],
            axis=dim,
        )
    return cells


def exchange(blocks, axes, collective_id):
    sizes = [lax.axis_size(axis) for axis in axes]
    count = math.prod(sizes)
    share = count // blocks.shape[0]

    def place(index):
        found = {}
        for axis, size in reversed(list(zip(axes, sizes))):
            found[axis] = lax.rem(index, size)
            index = index // size
        return found

    def kernel(x_ref, y_ref, own_sem, send_sem, recv_sem):
        me = 0
        for axis, size in zip(axes, sizes):
            me = me * size + lax.axis_index(axis)
        barrier = pltpu.get_barrier_semaphore()

        def copy(step):
            peer = lax.rem(me + step, count)
            return pltpu.make_async_remote_copy(
                src_ref=x_ref.at[peer // share],
                dst_ref=y_ref.at[me],
                send_sem=send_sem.at[step],
                recv_sem=recv_sem.at[step],
                device_id=place(peer),
                device_id_type=pl.DeviceIdType.MESH,
            )

        @pl.loop(1, count)
        def _(step):
            pl.semaphore_signal(
                barrier,
                inc=1,
                device_id=place(lax.rem(me + step, count)),
                device_id_type=pl.DeviceIdType.MESH,
            )

        pl.semaphore_wait(barrier, count - 1)

        @pl.loop(1, count)
        def _(step):
            copy(step).start()

        own = pltpu.make_async_copy(x_ref.at[me // share], y_ref.at[me], own_sem)
        own.start()
        own.wait()

        @pl.loop(1, count)
        def _(step):
            copy(step).wait()

    return pl.pallas_call(
        kernel,
        out_shape=jax.ShapeDtypeStruct((count,) + blocks.shape[1:], blocks.dtype),
        in_specs=[pl.BlockSpec(memory_space=pl.ANY)],
        out_specs=pl.BlockSpec(memory_space=pl.ANY),
        scratch_shapes=[
            pltpu.SemaphoreType.DMA,
            pltpu.SemaphoreType.DMA((count,)),
            pltpu.SemaphoreType.DMA((count,)),
        ],
        compiler_params=pltpu.CompilerParams(collective_id=collective_id, has_side_effects=True),
    )(blocks)


def line_gather(block, axis, pieces, collective_id):
    count = lax.axis_size(axis)
    rows = block.shape[0] // pieces

    def kernel(x_ref, y_ref, own_sem, send_sem, recv_sem):
        me = lax.axis_index(axis)
        barrier = pltpu.get_barrier_semaphore()
        has_left, has_right = me > 0, me < count - 1

        def signal(peer):
            pl.semaphore_signal(
                barrier, inc=1, device_id={axis: peer}, device_id_type=pl.DeviceIdType.MESH
            )

        @pl.when(has_left)
        def _():
            signal(me - 1)

        @pl.when(has_right)
        def _():
            signal(me + 1)

        pl.semaphore_wait(barrier, has_left.astype(jnp.int32) + has_right.astype(jnp.int32))

        def copy(source, piece, peer, way, own):
            part = pl.ds(piece * rows, rows)
            return pltpu.make_async_remote_copy(
                src_ref=x_ref.at[part] if own else y_ref.at[source, part],
                dst_ref=y_ref.at[source, part],
                send_sem=send_sem.at[way, source, piece],
                recv_sem=recv_sem.at[source, piece],
                device_id={axis: peer},
                device_id_type=pl.DeviceIdType.MESH,
            )

        for piece in range(pieces):

            @pl.when(has_right)
            def _():
                copy(me, piece, me + 1, 0, True).start()

            @pl.when(has_left)
            def _():
                copy(me, piece, me - 1, 1, True).start()

        own = pltpu.make_async_copy(x_ref, y_ref.at[me], own_sem)
        own.start()
        for step in range(1, count):
            for piece in range(pieces):

                @pl.when(me - step >= 0)
                def _():
                    copy(me - step, piece, me - 1, 0, False).wait_recv()

                    @pl.when(has_right)
                    def _():
                        copy(me - step, piece, me + 1, 0, False).start()

                @pl.when(me + step < count)
                def _():
                    copy(me + step, piece, me + 1, 1, False).wait_recv()

                    @pl.when(has_left)
                    def _():
                        copy(me + step, piece, me - 1, 1, False).start()

        own.wait()
        for step in range(count):
            for piece in range(pieces):

                @pl.when((me - step >= 0) & has_right)
                def _():
                    copy(me - step, piece, me + 1, 0, step == 0).wait_send()

                @pl.when((me + step < count) & has_left)
                def _():
                    copy(me + step, piece, me - 1, 1, step == 0).wait_send()

    return pl.pallas_call(
        kernel,
        out_shape=jax.ShapeDtypeStruct((count,) + block.shape, block.dtype),
        in_specs=[pl.BlockSpec(memory_space=pl.ANY)],
        out_specs=pl.BlockSpec(memory_space=pl.ANY),
        scratch_shapes=[
            pltpu.SemaphoreType.DMA,
            pltpu.SemaphoreType.DMA((2, count, pieces)),
            pltpu.SemaphoreType.DMA((count, pieces)),
        ],
        compiler_params=pltpu.CompilerParams(collective_id=collective_id, has_side_effects=True),
    )(block)


def rms_scaled(values, norm_gain):
    mean_square = jnp.mean(values * values, axis=-1, keepdims=True)
    return (values * lax.rsqrt(mean_square + EPSILON) * norm_gain).astype(jnp.bfloat16)


def masked_attend(query_rows, key_rows, value_rows, allowed, score_scale):
    scores = (
        jnp.einsum("qhd,nhd->hqn", query_rows, key_rows, preferred_element_type=jnp.float32)
        * score_scale
    )
    scores = jnp.where(allowed[None], scores, NEG_FILL)
    highest = jnp.max(scores, axis=-1, keepdims=True)
    weights_raw = jnp.where(allowed[None], jnp.exp(scores - highest), 0.0)
    totals = jnp.sum(weights_raw, axis=-1)
    mixed = jnp.einsum(
        "hqn,nhd->qhd",
        weights_raw.astype(jnp.bfloat16),
        value_rows,
        preferred_element_type=jnp.float32,
    )
    mixed = mixed / jnp.transpose(totals)[:, :, None]
    return mixed.reshape(mixed.shape[0], -1).astype(jnp.bfloat16)


def body(
    patches,
    image_ids,
    vision_gain,
    v_query,
    v_key,
    v_value,
    v_out,
    merge_gain,
    merge_up,
    merge_down,
    owners,
    text_embed,
    segment_ids,
    lang_gain,
    l_query,
    l_key,
    l_value,
    l_out,
):
    seq_count, tp_count = lax.axis_size("seq"), lax.axis_size("tp")
    seq_index, tp_index = lax.axis_index("seq"), lax.axis_index("tp")
    row_count = patches.shape[0]
    local_width = v_query.shape[1]
    head_size = DV // VHEADS
    head_count = local_width // head_size
    score_scale = 1.0 / math.sqrt(head_size)

    out_rows = v_out.shape[0] // seq_count
    v_out_whole = lax.all_gather(
        lax.dynamic_slice_in_dim(v_out, seq_index * out_rows, out_rows),
        ("tp", "seq"),
        axis=0,
        tiled=True,
    )

    patch_ids = jnp.repeat(image_ids, 4)
    my_ids = lax.dynamic_slice_in_dim(patch_ids, seq_index * row_count, row_count)
    normed = rms_scaled(patches.astype(jnp.float32), vision_gain)
    query_rows = jnp.dot(normed, v_query, preferred_element_type=jnp.float32).astype(jnp.bfloat16)
    key_part = jnp.dot(normed, v_key, preferred_element_type=jnp.float32).astype(jnp.bfloat16)
    value_part = jnp.dot(normed, v_value, preferred_element_type=jnp.float32).astype(jnp.bfloat16)
    key_value = jnp.concatenate([key_part, value_part], axis=1)
    query_grid = query_rows.reshape(row_count, head_count, head_size)
    nearby = extended(key_value, (("seq", 0),), row_count)
    padded_ids = jnp.pad(patch_ids, (row_count, row_count), constant_values=-1)
    nearby_ids = lax.dynamic_slice_in_dim(padded_ids, seq_index * row_count, 3 * row_count)
    allowed = my_ids[:, None] == nearby_ids[None, :]
    nearby_keys = nearby[:, :local_width].reshape(3 * row_count, head_count, head_size)
    nearby_values = nearby[:, local_width:].reshape(3 * row_count, head_count, head_size)
    attended = masked_attend(query_grid, nearby_keys, nearby_values, allowed, score_scale)

    own_rows = row_count // tp_count
    attended = exchange(attended.reshape(tp_count, own_rows, local_width), ("tp",), 0)
    attended = jnp.swapaxes(attended, 0, 1).reshape(own_rows, DV)
    own_patches = lax.dynamic_slice_in_dim(patches, tp_index * own_rows, own_rows)
    vision_state = own_patches.astype(jnp.float32) + jnp.dot(
        attended, v_out_whole, preferred_element_type=jnp.float32
    )
    merge_rows = rms_scaled(vision_state, merge_gain).reshape(own_rows // 4, 4 * DV)

    own_tokens = own_rows // 4
    merge_blocks = jnp.swapaxes(merge_rows.reshape(own_tokens, seq_count, -1), 0, 1)
    spread = exchange(merge_blocks, ("seq", "tp"), 1)
    spread = spread.reshape(seq_count * tp_count * own_tokens, -1)
    up_terms = jnp.dot(spread, merge_up, preferred_element_type=jnp.float32)
    token_count = row_count // 4
    up_terms = up_terms.astype(jnp.bfloat16).reshape(seq_count, token_count, -1)
    hidden_sum = jnp.sum(exchange(up_terms, ("seq",), 2).astype(jnp.float32), axis=0)
    hidden = jax.nn.gelu(hidden_sum, approximate=False).astype(jnp.bfloat16)
    hidden = lax.all_gather(hidden, "seq", axis=0, tiled=True)
    down_terms = jnp.dot(hidden, merge_down, preferred_element_type=jnp.float32)
    merged = lax.psum_scatter(
        down_terms.astype(jnp.bfloat16), "tp", scatter_dimension=1, tiled=True
    )

    slot_count = text_embed.shape[0]
    destination = owners[:, 0]
    one_hot = (
        destination[:, None] == jnp.arange(seq_count, dtype=jnp.int32)[None, :]
    ).astype(jnp.int32)
    rank = jnp.sum((jnp.cumsum(one_hot, axis=0) - one_hot) * one_hot, axis=1)
    slot = destination * slot_count + rank
    all_slots = jnp.arange(seq_count * slot_count, dtype=jnp.int32)
    slot_place = (all_slots[:, None] == slot[None, :]).astype(jnp.bfloat16)
    outgoing = jnp.dot(slot_place, merged, preferred_element_type=jnp.float32).astype(jnp.bfloat16)
    incoming = exchange(outgoing.reshape(seq_count, slot_count, -1), ("seq",), 3)
    own_width = text_embed.shape[1]
    vision_part = jnp.swapaxes(incoming, 0, 1).reshape(slot_count, own_width)
    vision_count = jnp.sum((destination == seq_index).astype(jnp.int32))
    slots = jnp.arange(slot_count, dtype=jnp.int32)
    is_vision = (slots < vision_count)[:, None]

    parts = line_gather(jnp.where(is_vision, vision_part, text_embed), "tp", 8, 4)
    text_order = jnp.swapaxes(parts, 0, 1).reshape(slot_count, -1)
    vision_order = jnp.transpose(
        parts.reshape(tp_count, slot_count, seq_count, -1), (1, 2, 0, 3)
    ).reshape(slot_count, -1)
    full_rows = jnp.where(is_vision, vision_order, text_order)
    filled = lax.dynamic_slice_in_dim(full_rows, tp_index * own_width, own_width, axis=1)

    lang_normed = lax.optimization_barrier(
        rms_scaled(full_rows.astype(jnp.float32), lang_gain)
    )
    lang_query = jnp.dot(lang_normed, l_query, preferred_element_type=jnp.float32).astype(
        jnp.bfloat16
    )
    lang_key = jnp.dot(lang_normed, l_key, preferred_element_type=jnp.float32).astype(jnp.bfloat16)
    lang_value = jnp.dot(lang_normed, l_value, preferred_element_type=jnp.float32).astype(
        jnp.bfloat16
    )
    kv_heads = l_key.shape[1] // LHD
    group_size = l_query.shape[1] // LHD // kv_heads
    query_five = lang_query.reshape(slot_count, kv_heads, group_size, LHD)
    key_three = lang_key.reshape(slot_count, kv_heads, LHD)
    value_three = lang_value.reshape(slot_count, kv_heads, LHD)
    allowed_lang = (segment_ids[:, None] == segment_ids[None, :]) & (
        slots[None, :] <= slots[:, None]
    )
    scores = jnp.einsum(
        "qkgd,nkd->kgqn", query_five, key_three, preferred_element_type=jnp.float32
    ) / math.sqrt(LHD)
    scores = jnp.where(allowed_lang[None, None], scores, NEG_FILL)
    highest = jnp.max(scores, axis=-1, keepdims=True)
    weights_raw = jnp.where(allowed_lang[None, None], jnp.exp(scores - highest), 0.0)
    totals = jnp.sum(weights_raw, axis=-1)
    mixed = jnp.einsum(
        "kgqn,nkd->qkgd",
        weights_raw.astype(jnp.bfloat16),
        value_three,
        preferred_element_type=jnp.float32,
    )
    mixed = mixed / jnp.transpose(totals, (2, 0, 1))[..., None]
    lang_attended = mixed.reshape(slot_count, -1).astype(jnp.bfloat16)
    lang_attended = lax.optimization_barrier(lang_attended)
    out_terms = jnp.dot(lang_attended, l_out, preferred_element_type=jnp.float32)
    summed_out = lax.psum_scatter(
        out_terms.astype(jnp.bfloat16), "tp", scatter_dimension=1, tiled=True
    ).astype(jnp.float32)
    return (filled.astype(jnp.float32) + summed_out).astype(jnp.bfloat16)


def solution(mesh):
    in_specs = (
        P("seq", None),
        P(),
        P(),
        P(None, "tp"),
        P(None, "tp"),
        P(None, "tp"),
        P("tp", None),
        P(),
        P("seq", "tp"),
        P("tp", "seq"),
        P(),
        P("seq", "tp"),
        P("seq"),
        P(),
        P(None, "tp"),
        P(None, "tp"),
        P(None, "tp"),
        P("tp", None),
    )
    out_specs = P("seq", "tp")
    return jax.shard_map(body, mesh=mesh, in_specs=in_specs, out_specs=out_specs, check_vma=False)
```
